32 devices in a mesh: rows: 8 (over y, x, core), section: 4 (over z).
Axes of the slice: x: 2, y: 2, z: 4, core: 2. Of those that a mesh axis runs over, the one named last changes fastest.
Arguments:
- start_vec: float32 [16384, 2, 256], P('rows'), may hold values from -6 to 6
- left_vec: float32 [16384, 2, 256], P('rows'), may hold values from -6 to 6
- hamil: bfloat16 [128, 16, 2, 128, 128], P('rows', 'section'), may hold values from -0.109375 to 0.109375
- cols: int32 [128, 16], P('rows', 'section'), may hold values from 0 to 127, as said below
- live: int32 [128, 4], P('rows', 'section'), may hold values from 1 to 4, as said below
Outputs:
- moments: float32 [5, 256], replicated
- last_vec: float32 [16384, 2, 256], P('rows')
- before_vec: float32 [16384, 2, 256], P('rows')
The draws below stay inside these ranges and needn't reach their ends.
Inputs may be any that keep to these rules, and one draw needn't show every extreme that they name: `cols`: each block column lies within 16 of its block row; slot 0 of every block row is the block row itself; a column may repeat in a row, and then its blocks add. `live`: loads differ between row groups.
All inputs are finite; a program needn't handle non-finite values.
Results may differ from the reference program's by a relative error of at most 0.0028.
Values may be sent and summed in bfloat16 or wider, within the bound.
A program may use at most 128 MiB of HBM per device.

```python
import jax
import jax.numpy as jnp
from jax import lax

BLOCK = 128
COLS = 256
RB_DEV = 16
REACH = 16
NNZ_ST = 4
STEPS = 4
NB = 128
SLOTS = 16
ORB = 16384
N_SECTION = 4


def draw_cols(key, part):
    offsets = jax.random.randint(key, (NB, SLOTS), -REACH, REACH + 1)
    offsets = offsets.at[:, 0].set(0)
    row_ids = jnp.arange(NB)[:, None]
    return jnp.clip(row_ids + offsets, 0, NB - 1).astype(jnp.int32)


def draw_live(key, part):
    base = jax.random.randint(key, (NB, N_SECTION), 1, NNZ_ST + 1)
    row_ids = jnp.arange(NB)[:, None]
    group = row_ids // RB_DEV
    dense = group % 3 == 0
    sparse_row = jnp.logical_and(group % 3 != 0, row_ids % RB_DEV == RB_DEV - 1)
    result = jnp.where(dense, NNZ_ST, jnp.where(sparse_row, 1, base))
    return result.astype(jnp.int32)


def levels(key, extent, cuts, least, high):
    loudness = 1.0
    for position, parts in cuts:
        heights = jax.random.uniform(jax.random.fold_in(jax.random.fold_in(key, 6), position), (parts,), jnp.float32, least / len(cuts), high / len(cuts))
        loudness = loudness * jnp.repeat(jnp.exp(heights), extent[position] // parts).reshape((-1,) + (1,) * (len(extent) - 1 - position))
    return loudness


def normal_values(own_key, dims, deviation, bound, split=(), kind=jnp.bfloat16):
    entries = deviation * jax.random.normal(own_key, dims, jnp.float32)
    if split:
        entries = entries * levels(own_key, dims, split, -0.22, 0.18)
    return jnp.clip(entries, -bound, bound).astype(kind)


def setup_inputs(seed: int = 0) -> dict:
    streams_of = jax.random.split(jax.random.key(seed), 6)
    return {
        "start_vec": normal_values(streams_of[0], (ORB, 2, COLS), 1.0, 6.0, ((0, 8),), jnp.float32),
        "left_vec": normal_values(streams_of[1], (ORB, 2, COLS), 1.0, 6.0, ((0, 8),), jnp.float32),
        "hamil": normal_values(streams_of[2], (NB, SLOTS, 2, BLOCK, BLOCK), (0.45 / (2 * BLOCK * SLOTS) ** 0.5), 0.109375, ((0, 8), (1, 4))),
        "cols": draw_cols(jax.random.fold_in(streams_of[5], 71), 0),
        "live": draw_live(jax.random.fold_in(streams_of[5], 71), 0),
    }


def reference(start_vec, left_vec, hamil, cols, live):
    slot_ids = jnp.arange(SLOTS)
    segment_of = slot_ids // NNZ_ST
    within = slot_ids % NNZ_ST
    mask = (within[None, :] < live[:, segment_of]).astype(jnp.float32)
    scale = 1.0 / (2.0 * BLOCK * RB_DEV) ** 0.5

    def product(vec):
        rounded = lax.optimization_barrier(vec.astype(jnp.bfloat16))
        blocks = rounded.astype(jnp.float32).reshape(NB, BLOCK, 2, COLS)

        def one_row(items):
            matrix, columns, marks = items
            panels = blocks[columns] * marks[:, None, None, None]
            out = jnp.einsum("kqij,kjpc->qipc", matrix.astype(jnp.float32), panels,
                             precision=lax.Precision.HIGHEST)
            real_part = out[0, :, 0] - out[1, :, 1]
            imag_part = out[0, :, 1] + out[1, :, 0]
            return jnp.stack([real_part, imag_part], axis=1)

        return lax.map(one_row, (hamil, cols, mask)).reshape(NB * BLOCK, 2, COLS)

    def moment(vec):
        return jnp.sum(left_vec * vec, axis=(0, 1)) * scale

    current = start_vec
    previous = start_vec
    table = [moment(current)]
    for step in range(STEPS):
        summed = product(current)
        if step == 0:
            fresh = summed
        else:
            fresh = 2.0 * summed - previous
        previous, current = current, fresh
        table.append(moment(current))
    return jnp.stack(table, axis=0), current, previous
```

```python
import functools

import jax
import jax.numpy as jnp
from jax import lax
from jax.experimental import pallas as pl
from jax.experimental.pallas import tpu as pltpu
from jax.sharding import PartitionSpec as P

MESH = pl.DeviceIdType.MESH
STEPS = 4
GROUP = 16


def kernel(
    nr, ns, slots, scale,
    idx, v0, own0, left, hm,
    mom_out, t3_out, t4_out,
    ext0, ext1, ext2, ext3, last, hrecv, hc, tbuf, mloc, msec, mrow,
    up_sem, down_sem, right_sem, left_sem, own_recv, lhalo_recv, rhalo_recv,
    h_send, h_recv, m_send, m_recv, n_send, n_recv, local_sem,
):
    g = lax.axis_index("rows")
    s = lax.axis_index("section")
    rb = v0.shape[0]
    R = rb // ns
    bs = hm.shape[-1]
    sc = hm.shape[1]
    bufs = (ext0, ext1, ext2, ext3, last)

    barrier = pltpu.get_barrier_semaphore()

    @pl.loop(1, ns)
    def _(d):
        pl.semaphore_signal(barrier, inc=1, device_id=(g, lax.rem(s + d, ns)), device_id_type=MESH)

    @pl.loop(1, nr)
    def _(d):
        pl.semaphore_signal(barrier, inc=1, device_id=(lax.rem(g + d, nr), s), device_id_type=MESH)

    pl.semaphore_wait(barrier, ns + nr - 2)

    def own(n, c):
        return bufs[n].at[c] if n == STEPS else bufs[n].at[rb + c]

    def remote(src, dst, ss, rs, dev):
        return pltpu.make_async_remote_copy(
            src_ref=src, dst_ref=dst, send_sem=ss, recv_sem=rs, device_id=dev, device_id_type=MESH
        )

    def up(n, c):
        return remote(own(n, c), own(n, c), up_sem.at[n - 1, c], own_recv.at[n - 1, c], (g, s + 1))

    def down(n, c):
        return remote(own(n, c), own(n, c), down_sem.at[n - 1, c], own_recv.at[n - 1, c], (g, s - 1))

    def right(n, c):
        src = v0.at[c] if n == 0 else own(n, c)
        return remote(src, bufs[n].at[c], right_sem.at[n, c], lhalo_recv.at[n, c], (g + 1, s))

    def leftward(n, c):
        src = v0.at[c] if n == 0 else own(n, c)
        return remote(src, bufs[n].at[2 * rb + c], left_sem.at[n, c], rhalo_recv.at[n, c], (g - 1, s))

    def each(n, c, act):
        k = c // R
        if n > 0:
            @pl.when((k <= s) & (s < ns - 1))
            def _():
                act(up(n, c))

            @pl.when((k >= s) & (s > 0))
            def _():
                act(down(n, c))
        if n < STEPS:
            @pl.when((k >= s) & (g < nr - 1))
            def _():
                act(right(n, c))

            @pl.when((k <= s) & (g > 0))
            def _():
                act(leftward(n, c))

    def halos(n):
        @pl.loop(0, rb)
        def _(c):
            k = c // R

            @pl.when((k >= s) & (g > 0))
            def _():
                right(n, c).wait_recv()

            @pl.when((k <= s) & (g < nr - 1))
            def _():
                leftward(n, c).wait_recv()

    def coupling(d, r):
        to = lax.rem(s + d, ns)
        return remote(hm.at[to * R + r], hrecv.at[s, r], h_send.at[to, r], h_recv.at[s, r], (g, to))

    def arrived(d, r):
        at = lax.rem(s + d, ns)
        return remote(hm.at[r], hrecv.at[at, r], h_send.at[at, r], h_recv.at[at, r], (g, at))

    @pl.loop(0, R)
    def _(r):
        @pl.loop(1, ns)
        def _(d):
            coupling(d, r).start()

    @pl.loop(0, rb)
    def _(c):
        each(0, c, lambda x: x.start())

    copy_h = pltpu.make_async_copy(hm.at[pl.ds(s * R, R)], hrecv.at[s], local_sem.at[0])
    copy_v = pltpu.make_async_copy(v0, ext0.at[pl.ds(rb, rb)], local_sem.at[1])
    copy_h.start()
    copy_v.start()
    mloc[...] = jnp.zeros_like(mloc)

    def moment(n, r, t):
        mloc[n : n + 1, :] += jnp.sum(left[r] * t, axis=0, keepdims=True)

    @pl.loop(0, R)
    def _(r):
        moment(0, r, own0[r])
        tbuf[0, r] = own0[r]

    copy_h.wait()
    copy_v.wait()
    halos(0)

    def build(r):
        @pl.loop(0, slots)
        def _(j):
            src, k = j // sc, j % sc
            hr = hrecv[src, r, k, 0]
            hi = hrecv[src, r, k, 1]
            first = pl.ds(pl.multiple_of(j * 2 * bs, bs), bs)
            second = pl.ds(pl.multiple_of(j * 2 * bs + bs, bs), bs)
            hc[r, 0:bs, first] = hr
            hc[r, 0:bs, second] = -hi
            hc[r, bs : 2 * bs, first] = hi
            hc[r, bs : 2 * bs, second] = hr

    group = min(GROUP, slots)

    def product(n, r):
        def part(p):
            base = p * group
            rhs = jnp.concatenate(
                [bufs[n - 1][idx[r * slots + base + u]] for u in range(group)], axis=0
            )
            lhs = hc[r, :, pl.ds(pl.multiple_of(base * 2 * bs, 2 * bs), group * 2 * bs)]
            return jnp.dot(lhs, rhs, preferred_element_type=jnp.float32)

        if slots == group:
            return part(0)
        zero = jnp.zeros((2 * bs, v0.shape[-1]), jnp.float32)
        return lax.fori_loop(0, slots // group, lambda p, a: a + part(p), zero)

    for n in range(1, STEPS + 1):
        @pl.loop(0, R)
        def _(r, n=n):
            if n == 1:
                @pl.loop(1, ns)
                def _(d):
                    arrived(d, r).wait_recv()

                build(r)
            t = product(n, r)
            if n > 1:
                t = 2.0 * t - tbuf[n % 2, r]
            tbuf[n % 2, r] = t
            c = s * R + r
            if n == STEPS:
                bufs[n][c] = t.astype(jnp.bfloat16)
            else:
                bufs[n][rb + c] = t.astype(jnp.bfloat16)
            each(n, c, lambda x: x.start())
            moment(n, r, t)

        if n == STEPS:
            msec[s] = mloc[...]

            @pl.loop(1, ns)
            def _(d):
                to = lax.rem(s + d, ns)
                remote(mloc, msec.at[s], m_send.at[to], m_recv.at[s], (g, to)).start()

        @pl.loop(1, ns)
        def _(d, n=n):
            @pl.loop(0, R)
            def _(r):
                @pl.when(s - d >= 0)
                def _():
                    c = (s - d) * R + r
                    up(n, c).wait_recv()
                    each(n, c, lambda x: x.start())

                @pl.when(s + d < ns)
                def _():
                    c = (s + d) * R + r
                    down(n, c).wait_recv()
                    each(n, c, lambda x: x.start())

        if n < STEPS:
            halos(n)
        if n == STEPS - 1:
            pltpu.make_async_copy(ext3.at[pl.ds(rb, rb)], t3_out, local_sem.at[2]).start()

    copy_t = pltpu.make_async_copy(last, t4_out, local_sem.at[3])
    copy_t.start()

    @pl.loop(1, ns)
    def _(d):
        at = lax.rem(s + d, ns)
        remote(mloc, msec.at[at], m_send.at[at], m_recv.at[at], (g, at)).wait()

    total = msec[0]
    for i in range(1, ns):
        total += msec[i]
    mrow[g] = total

    @pl.loop(1, nr)
    def _(d):
        to = lax.rem(g + d, nr)
        remote(mrow.at[g], mrow.at[g], n_send.at[to], n_recv.at[g], (to, s)).start()

    @pl.loop(1, nr)
    def _(d):
        at = lax.rem(g + d, nr)
        remote(mrow.at[at], mrow.at[at], n_send.at[at], n_recv.at[at], (at, s)).wait()

    total = mrow[0]
    for i in range(1, nr):
        total += mrow[i]
    mom_out[...] = total * scale

    @pl.loop(0, R)
    def _(r):
        @pl.loop(1, ns)
        def _(d):
            coupling(d, r).wait_send()

    for n in range(STEPS + 1):
        @pl.loop(0, rb)
        def _(c, n=n):
            each(n, c, lambda x: x.wait_send())

    pltpu.make_async_copy(ext3.at[pl.ds(rb, rb)], t3_out, local_sem.at[2]).wait()
    copy_t.wait()


def body(nr, ns, start_vec, left_vec, hamil, cols, live):
    rb, sc = cols.shape
    bs = hamil.shape[-1]
    width = start_vec.shape[-1]
    R = rb // ns
    slots = sc * ns
    s = lax.axis_index("section")
    base = lax.axis_index("rows") * rb
    scale = 1.0 / (2.0 * bs * rb) ** 0.5

    def panels(x):
        count = x.shape[0] // bs
        return x.reshape(count, bs, 2, width).transpose(0, 2, 1, 3).reshape(count, 2 * bs, width)

    def owned(x):
        return panels(lax.dynamic_slice_in_dim(x, s * (R * bs), R * bs, axis=0))

    v0 = panels(start_vec.astype(jnp.bfloat16))
    mask = jnp.arange(sc)[None, :] < live
    hm = jnp.where(mask[:, :, None, None, None], hamil, jnp.zeros((), hamil.dtype))
    every = lax.all_gather(cols, "section", axis=1, tiled=True)
    idx = (lax.dynamic_slice_in_dim(every, s * R, R, axis=0) - base + rb).reshape(-1)

    dma = pltpu.SemaphoreType.DMA
    vmem = pl.BlockSpec(memory_space=pltpu.VMEM)
    anywhere = pl.BlockSpec(memory_space=pl.ANY)
    bf, f32 = jnp.bfloat16, jnp.float32
    ext = pltpu.VMEM((3 * rb, 2 * bs, width), bf)
    mom, t3, t4 = pl.pallas_call(
        functools.partial(kernel, nr, ns, slots, scale),
        out_shape=(
            jax.ShapeDtypeStruct((8, width), f32),
            jax.ShapeDtypeStruct((rb, 2 * bs, width), bf),
            jax.ShapeDtypeStruct((rb, 2 * bs, width), bf),
        ),
        in_specs=[pl.BlockSpec(memory_space=pltpu.SMEM), anywhere, vmem, vmem, anywhere],
        out_specs=(vmem, anywhere, anywhere),
        scratch_shapes=[
            ext, ext, ext, ext,
            pltpu.VMEM((rb, 2 * bs, width), bf),
            pltpu.VMEM((ns, R, sc, 2, bs, bs), bf),
            pltpu.VMEM((R, 2 * bs, slots * 2 * bs), bf),
            pltpu.VMEM((2, R, 2 * bs, width), f32),
            pltpu.VMEM((8, width), f32),
            pltpu.VMEM((ns, 8, width), f32),
            pltpu.VMEM((nr, 8, width), f32),
            dma((STEPS, rb)), dma((STEPS, rb)), dma((STEPS, rb)), dma((STEPS, rb)),
            dma((STEPS, rb)), dma((STEPS, rb)), dma((STEPS, rb)),
            dma((ns, R)), dma((ns, R)),
            dma((ns,)), dma((ns,)), dma((nr,)), dma((nr,)), dma((4,)),
        ],
        compiler_params=pltpu.CompilerParams(
            collective_id=0, has_side_effects=True, vmem_limit_bytes=56 * 2**20
        ),
    )(idx, v0, owned(start_vec), owned(left_vec), hm)

    def whole(x):
        return (
            x.astype(f32).reshape(rb, 2, bs, width).transpose(0, 2, 1, 3).reshape(rb * bs, 2, width)
        )

    return mom[: STEPS + 1], whole(t4), whole(t3)


def solution(mesh):
    nr, ns = mesh.shape["rows"], mesh.shape["section"]
    return jax.shard_map(
        functools.partial(body, nr, ns),
        mesh=mesh,
        in_specs=(
            P("rows", None, None),
            P("rows", None, None),
            P("rows", "section", None, None, None),
            P("rows", "section"),
            P("rows", "section"),
        ),
        out_specs=(P(), P("rows", None, None), P("rows", None, None)),
        check_vma=False,
    )
```

```python
import functools

import jax
import jax.numpy as jnp
from jax import lax
from jax.experimental import pallas as pl
from jax.experimental.pallas import tpu as pltpu
from jax.sharding import PartitionSpec as P

MESH = pl.DeviceIdType.MESH
STEPS = 4
GROUP = 16


def kernel(
    nr, ns, slots, scale,
    code, start_hbm, left_hbm, hm,
    mom_out, t3_out, t4_out,
    stage, left_stage, codes, idx, ext0, ext1, ext2, ext3, last, hrecv, hc, tbuf, left, mloc, msec, mrow,
    up_sem, down_sem, right_sem, left_sem, own_recv, lhalo_recv, rhalo_recv,
    h_send, h_recv, c_send, c_recv, m_send, m_recv, n_send, n_recv, local_sem,
):
    g = lax.axis_index("rows")
    s = lax.axis_index("section")
    rb = hm.shape[0]
    width = start_hbm.shape[-1]
    R = rb // ns
    bs = hm.shape[-1]
    sc = hm.shape[1]
    bufs = (ext0, ext1, ext2, ext3, last)

    barrier = pltpu.get_barrier_semaphore()

    @pl.loop(1, ns)
    def _(d):
        pl.semaphore_signal(barrier, inc=1, device_id=(g, lax.rem(s + d, ns)), device_id_type=MESH)

    @pl.loop(1, nr)
    def _(d):
        pl.semaphore_signal(barrier, inc=1, device_id=(lax.rem(g + d, nr), s), device_id_type=MESH)

    pl.semaphore_wait(barrier, ns + nr - 2)

    def own(n, c):
        return bufs[n].at[c] if n == STEPS else bufs[n].at[rb + c]

    def remote(src, dst, ss, rs, dev):
        return pltpu.make_async_remote_copy(
            src_ref=src, dst_ref=dst, send_sem=ss, recv_sem=rs, device_id=dev, device_id_type=MESH
        )

    def up(n, c):
        return remote(own(n, c), own(n, c), up_sem.at[n - 1, c], own_recv.at[n - 1, c], (g, s + 1))

    def down(n, c):
        return remote(own(n, c), own(n, c), down_sem.at[n - 1, c], own_recv.at[n - 1, c], (g, s - 1))

    def right(n, c):
        return remote(own(n, c), bufs[n].at[c], right_sem.at[n, c], lhalo_recv.at[n, c], (g + 1, s))

    def leftward(n, c):
        return remote(own(n, c), bufs[n].at[2 * rb + c], left_sem.at[n, c], rhalo_recv.at[n, c], (g - 1, s))

    def each(n, c, act):
        k = c // R
        if n > 0:
            @pl.when((k <= s) & (s < ns - 1))
            def _():
                act(up(n, c))

            @pl.when((k >= s) & (s > 0))
            def _():
                act(down(n, c))
        if n < STEPS:
            @pl.when((k >= s) & (g < nr - 1))
            def _():
                act(right(n, c))

            @pl.when((k <= s) & (g > 0))
            def _():
                act(leftward(n, c))

    def halos(n):
        @pl.loop(0, rb)
        def _(c):
            k = c // R

            @pl.when((k >= s) & (g > 0))
            def _():
                right(n, c).wait_recv()

            @pl.when((k <= s) & (g < nr - 1))
            def _():
                leftward(n, c).wait_recv()

    def coupling(d, r):
        to = lax.rem(s + d, ns)
        return remote(hm.at[to * R + r], hrecv.at[s, r], h_send.at[to, r], h_recv.at[s, r], (g, to))

    def arrived(d, r):
        at = lax.rem(s + d, ns)
        return remote(hm.at[r], hrecv.at[at, r], h_send.at[at, r], h_recv.at[at, r], (g, at))

    @pl.loop(1, ns)
    def _(d):
        to = lax.rem(s + d, ns)
        remote(code.at[to], codes.at[s], c_send.at[to], c_recv.at[s], (g, to)).start()

    ahead = min(2, R)
    for r in range(ahead):
        @pl.loop(1, ns)
        def _(d, r=r):
            coupling(d, r).start()

    copy_v = pltpu.make_async_copy(start_hbm, stage, local_sem.at[1])
    copy_v.start()
    copy_l = pltpu.make_async_copy(
        left_hbm.at[pl.ds(s * (R * bs), R * bs)], left_stage, local_sem.at[4]
    )
    copy_l.start()
    copy_h = pltpu.make_async_copy(hm.at[pl.ds(s * R, R)], hrecv.at[s], local_sem.at[0])
    copy_h.start()
    mloc[...] = jnp.zeros_like(mloc)
    codes[s] = code[s]
    copy_v.wait()

    @pl.loop(0, rb)
    def _(c):
        for q in range(2):
            part = stage[pl.ds(c * bs, bs), q, :]
            ext0[rb + c, q * bs : (q + 1) * bs, :] = part.astype(jnp.bfloat16)
        each(0, c, lambda x: x.start())

    copy_l.wait()

    def moment(n, r, t):
        for q in range(2):
            probe = left[r, q * bs : (q + 1) * bs, :]
            mloc[n : n + 1, :] += jnp.sum(probe * t[q * bs : (q + 1) * bs], axis=0, keepdims=True)

    @pl.loop(0, R)
    def _(r):
        for q in range(2):
            rows = slice(q * bs, (q + 1) * bs)
            tbuf[0, r, rows, :] = stage[pl.ds((s * R + r) * bs, bs), q, :]
            left[r, rows, :] = left_stage[pl.ds(r * bs, bs), q, :]
        moment(0, r, tbuf[0, r])

    @pl.loop(1, ns)
    def _(d):
        at = lax.rem(s + d, ns)
        remote(code.at[at], codes.at[at], c_send.at[at], c_recv.at[at], (g, at)).wait()

    copy_c = pltpu.make_async_copy(codes, idx, local_sem.at[5])
    copy_c.start()
    copy_c.wait()
    copy_h.wait()
    halos(0)

    def build(r):
        @pl.loop(0, slots)
        def _(j):
            src, k = j // sc, j % sc
            keep = jnp.where(idx[src, 0, r * sc + k] >= 0, 1.0, 0.0).astype(jnp.float32)
            hr = (hrecv[src, r, k, 0].astype(jnp.float32) * keep).astype(jnp.bfloat16)
            hi = (hrecv[src, r, k, 1].astype(jnp.float32) * keep).astype(jnp.bfloat16)
            first = pl.ds(pl.multiple_of(j * 2 * bs, bs), bs)
            second = pl.ds(pl.multiple_of(j * 2 * bs + bs, bs), bs)
            hc[r, 0:bs, first] = hr
            hc[r, 0:bs, second] = -hi
            hc[r, bs : 2 * bs, first] = hi
            hc[r, bs : 2 * bs, second] = hr

    group = min(GROUP, slots)

    def panel(r, j):
        at = idx[j // sc, 0, r * sc + j % sc]
        return jnp.where(at >= 0, at, rb)

    def product(n, r):
        def part(p):
            base = p * group
            rhs = jnp.concatenate(
                [bufs[n - 1][panel(r, base + u)] for u in range(group)], axis=0
            )
            lhs = hc[r, :, pl.ds(pl.multiple_of(base * 2 * bs, 2 * bs), group * 2 * bs)]
            return jnp.dot(lhs, rhs, preferred_element_type=jnp.float32)

        if slots == group:
            return part(0)
        zero = jnp.zeros((2 * bs, width), jnp.float32)
        return lax.fori_loop(0, slots // group, lambda p, a: a + part(p), zero)

    for n in range(1, STEPS + 1):
        @pl.loop(0, R)
        def _(r, n=n):
            if n == 1:
                @pl.loop(1, ns)
                def _(d):
                    arrived(d, r).wait_recv()

                @pl.when(r + ahead < R)
                def _():
                    @pl.loop(1, ns)
                    def _(d):
                        coupling(d, r).wait_send()

                    @pl.loop(1, ns)
                    def _(d):
                        coupling(d, r + ahead).start()

                build(r)
            t = product(n, r)
            if n > 1:
                t = 2.0 * t - tbuf[n % 2, r]
            tbuf[n % 2, r] = t
            c = s * R + r
            if n == STEPS:
                bufs[n][c] = t.astype(jnp.bfloat16)
            else:
                bufs[n][rb + c] = t.astype(jnp.bfloat16)
            each(n, c, lambda x: x.start())
            moment(n, r, t)

        if n == STEPS:
            msec[s] = mloc[...]

            @pl.loop(1, ns)
            def _(d):
                to = lax.rem(s + d, ns)
                remote(mloc, msec.at[s], m_send.at[to], m_recv.at[s], (g, to)).start()

        @pl.loop(1, ns)
        def _(d, n=n):
            @pl.loop(0, R)
            def _(r):
                @pl.when(s - d >= 0)
                def _():
                    c = (s - d) * R + r
                    up(n, c).wait_recv()
                    each(n, c, lambda x: x.start())

                @pl.when(s + d < ns)
                def _():
                    c = (s + d) * R + r
                    down(n, c).wait_recv()
                    each(n, c, lambda x: x.start())

        if n < STEPS:
            halos(n)
        if n == STEPS - 1:
            pltpu.make_async_copy(ext3.at[pl.ds(rb, rb)], t3_out, local_sem.at[2]).start()

    copy_t = pltpu.make_async_copy(last, t4_out, local_sem.at[3])
    copy_t.start()

    @pl.loop(1, ns)
    def _(d):
        at = lax.rem(s + d, ns)
        remote(mloc, msec.at[at], m_send.at[at], m_recv.at[at], (g, at)).wait()

    total = msec[0]
    for i in range(1, ns):
        total += msec[i]
    mrow[g] = total

    @pl.loop(1, nr)
    def _(d):
        to = lax.rem(g + d, nr)
        remote(mrow.at[g], mrow.at[g], n_send.at[to], n_recv.at[g], (to, s)).start()

    @pl.loop(1, nr)
    def _(d):
        at = lax.rem(g + d, nr)
        remote(mrow.at[at], mrow.at[at], n_send.at[at], n_recv.at[at], (at, s)).wait()

    total = mrow[0]
    for i in range(1, nr):
        total += mrow[i]
    mom_out[...] = total * scale

    for r in range(R - ahead, R):
        @pl.loop(1, ns)
        def _(d, r=r):
            coupling(d, r).wait_send()

    for n in range(STEPS + 1):
        @pl.loop(0, rb)
        def _(c, n=n):
            each(n, c, lambda x: x.wait_send())

    pltpu.make_async_copy(ext3.at[pl.ds(rb, rb)], t3_out, local_sem.at[2]).wait()
    copy_t.wait()


def widen(bs, t4, t3, last_vec, before_vec):
    for src, dst in ((t4, last_vec), (t3, before_vec)):
        for q in range(2):
            dst[:, q, :] = src[0, q * bs : (q + 1) * bs, :].astype(jnp.float32)


def body(nr, ns, start_vec, left_vec, hamil, cols, live):
    rb, sc = cols.shape
    bs = hamil.shape[-1]
    width = start_vec.shape[-1]
    R = rb // ns
    slots = sc * ns
    base = lax.axis_index("rows") * rb
    scale = 1.0 / (2.0 * bs * rb) ** 0.5

    mask = jnp.arange(sc)[None, :] < live
    code = jnp.where(mask, cols - base + rb, -1).reshape(ns, 1, R * sc)
    code = jnp.pad(code, ((0, 0), (0, 7), (0, -(R * sc) % 128)), constant_values=-1)

    dma = pltpu.SemaphoreType.DMA
    vmem = pl.BlockSpec(memory_space=pltpu.VMEM)
    anywhere = pl.BlockSpec(memory_space=pl.ANY)
    bf, f32 = jnp.bfloat16, jnp.float32
    ext = pltpu.VMEM((3 * rb, 2 * bs, width), bf)
    mom, t3, t4 = pl.pallas_call(
        functools.partial(kernel, nr, ns, slots, scale),
        out_shape=(
            jax.ShapeDtypeStruct((8, width), f32),
            jax.ShapeDtypeStruct((rb, 2 * bs, width), bf),
            jax.ShapeDtypeStruct((rb, 2 * bs, width), bf),
        ),
        in_specs=[vmem, anywhere, anywhere, anywhere],
        out_specs=(vmem, anywhere, anywhere),
        scratch_shapes=[
            pltpu.VMEM(start_vec.shape, f32),
            pltpu.VMEM((R * bs, 2, width), f32),
            pltpu.VMEM(code.shape, jnp.int32),
            pltpu.SMEM(code.shape, jnp.int32),
            ext, ext, ext, ext,
            pltpu.VMEM((rb, 2 * bs, width), bf),
            pltpu.VMEM((ns, R, sc, 2, bs, bs), bf),
            pltpu.VMEM((R, 2 * bs, slots * 2 * bs), bf),
            pltpu.VMEM((2, R, 2 * bs, width), f32),
            pltpu.VMEM((R, 2 * bs, width), f32),
            pltpu.VMEM((8, width), f32),
            pltpu.VMEM((ns, 8, width), f32),
            pltpu.VMEM((nr, 8, width), f32),
            dma((STEPS, rb)), dma((STEPS, rb)), dma((STEPS, rb)), dma((STEPS, rb)),
            dma((STEPS, rb)), dma((STEPS, rb)), dma((STEPS, rb)),
            dma((ns, R)), dma((ns, R)), dma((ns,)), dma((ns,)),
            dma((ns,)), dma((ns,)), dma((nr,)), dma((nr,)), dma((6,)),
        ],
        compiler_params=pltpu.CompilerParams(
            collective_id=0, has_side_effects=True, vmem_limit_bytes=56 * 2**20
        ),
    )(code, start_vec, left_vec, hamil)

    taken = pl.BlockSpec((1, 2 * bs, width), lambda b: (b, 0, 0))
    given = pl.BlockSpec((bs, 2, width), lambda b: (b, 0, 0))
    last_vec, before_vec = pl.pallas_call(
        functools.partial(widen, bs),
        out_shape=(jax.ShapeDtypeStruct(start_vec.shape, f32),) * 2,
        grid=(rb,),
        in_specs=[taken, taken],
        out_specs=(given, given),
    )(t4, t3)
    return mom[: STEPS + 1], last_vec, before_vec


def solution(mesh):
    nr, ns = mesh.shape["rows"], mesh.shape["section"]
    return jax.shard_map(
        functools.partial(body, nr, ns),
        mesh=mesh,
        in_specs=(
            P("rows", None, None),
            P("rows", None, None),
            P("rows", "section", None, None, None),
            P("rows", "section"),
            P("rows", "section"),
        ),
        out_specs=(P(), P("rows", None, None), P("rows", None, None)),
        check_vma=False,
    )
```

```python
import functools

import jax
import jax.numpy as jnp
from jax import lax
from jax.experimental import pallas as pl
from jax.experimental.pallas import tpu as pltpu
from jax.sharding import PartitionSpec as P

MESH = pl.DeviceIdType.MESH
STEPS = 4
GROUP = 16


def kernel(
    nr, ns, slots, scale,
    code, start_hbm, left_hbm, hm,
    mom_out, t3_out, t4_out,
    stage, left_stage, codes, idx, ext0, ext1, ext2, ext3, last, hrecv, hc, tbuf, left, mloc, msec, mrow,
    up_sem, down_sem, right_sem, left_sem, own_recv, lhalo_recv, rhalo_recv,
    h_send, h_recv, c_send, c_recv, m_send, m_recv, n_send, n_recv, local_sem,
):
    g = lax.axis_index("rows")
    s = lax.axis_index("section")
    rb = hm.shape[0]
    width = start_hbm.shape[-1]
    R = rb // ns
    bs = hm.shape[-1]
    sc = hm.shape[1]
    bufs = (ext0, ext1, ext2, ext3, last)

    barrier = pltpu.get_barrier_semaphore()

    @pl.loop(1, ns)
    def _(d):
        pl.semaphore_signal(barrier, inc=1, device_id=(g, lax.rem(s + d, ns)), device_id_type=MESH)

    @pl.loop(1, nr)
    def _(d):
        pl.semaphore_signal(barrier, inc=1, device_id=(lax.rem(g + d, nr), s), device_id_type=MESH)

    pl.semaphore_wait(barrier, ns + nr - 2)

    def own(n, c):
        return bufs[n].at[c] if n == STEPS else bufs[n].at[rb + c]

    def remote(src, dst, ss, rs, dev):
        return pltpu.make_async_remote_copy(
            src_ref=src, dst_ref=dst, send_sem=ss, recv_sem=rs, device_id=dev, device_id_type=MESH
        )

    def up(n, c):
        return remote(own(n, c), own(n, c), up_sem.at[n - 1, c], own_recv.at[n - 1, c], (g, s + 1))

    def down(n, c):
        return remote(own(n, c), own(n, c), down_sem.at[n - 1, c], own_recv.at[n - 1, c], (g, s - 1))

    def right(n, c):
        return remote(own(n, c), bufs[n].at[c], right_sem.at[n, c], lhalo_recv.at[n, c], (g + 1, s))

    def leftward(n, c):
        return remote(own(n, c), bufs[n].at[2 * rb + c], left_sem.at[n, c], rhalo_recv.at[n, c], (g - 1, s))

    def each(n, c, act):
        k = c // R
        if n > 0:
            @pl.when((k <= s) & (s < ns - 1))
            def _():
                act(up(n, c))

            @pl.when((k >= s) & (s > 0))
            def _():
                act(down(n, c))
        if n < STEPS:
            @pl.when((k >= s) & (g < nr - 1))
            def _():
                act(right(n, c))

            @pl.when((k <= s) & (g > 0))
            def _():
                act(leftward(n, c))

    def halos(n):
        @pl.loop(0, rb)
        def _(c):
            k = c // R

            @pl.when((k >= s) & (g > 0))
            def _():
                right(n, c).wait_recv()

            @pl.when((k <= s) & (g < nr - 1))
            def _():
                leftward(n, c).wait_recv()

    def coupling(d, r):
        to = lax.rem(s + d, ns)
        return remote(hm.at[to * R + r], hrecv.at[s, r], h_send.at[to, r], h_recv.at[s, r], (g, to))

    def arrived(d, r):
        at = lax.rem(s + d, ns)
        return remote(hm.at[r], hrecv.at[at, r], h_send.at[at, r], h_recv.at[at, r], (g, at))

    @pl.loop(1, ns)
    def _(d):
        to = lax.rem(s + d, ns)
        remote(code.at[to], codes.at[s], c_send.at[to], c_recv.at[s], (g, to)).start()

    ahead = min(4, R)
    for r in range(ahead):
        @pl.loop(1, ns)
        def _(d, r=r):
            coupling(d, r).start()

    copy_v = pltpu.make_async_copy(start_hbm, stage, local_sem.at[1])
    copy_v.start()
    copy_l = pltpu.make_async_copy(
        left_hbm.at[pl.ds(s * (R * bs), R * bs)], left_stage, local_sem.at[4]
    )
    copy_l.start()
    copy_h = pltpu.make_async_copy(hm.at[pl.ds(s * R, R)], hrecv.at[s], local_sem.at[0])
    copy_h.start()
    mloc[...] = jnp.zeros_like(mloc)
    codes[s] = code[s]
    copy_v.wait()

    @pl.loop(0, rb)
    def _(c):
        for q in range(2):
            part = stage[pl.ds(c * bs, bs), q, :]
            ext0[rb + c, q * bs : (q + 1) * bs, :] = part.astype(jnp.bfloat16)
        each(0, c, lambda x: x.start())

    copy_l.wait()

    def moment(n, r, t):
        for q in range(2):
            probe = left[r, q * bs : (q + 1) * bs, :]
            mloc[n : n + 1, :] += jnp.sum(probe * t[q * bs : (q + 1) * bs], axis=0, keepdims=True)

    @pl.loop(0, R)
    def _(r):
        for q in range(2):
            rows = slice(q * bs, (q + 1) * bs)
            tbuf[0, r, rows, :] = stage[pl.ds((s * R + r) * bs, bs), q, :]
            left[r, rows, :] = left_stage[pl.ds(r * bs, bs), q, :]
        moment(0, r, tbuf[0, r])

    @pl.loop(1, ns)
    def _(d):
        at = lax.rem(s + d, ns)
        remote(code.at[at], codes.at[at], c_send.at[at], c_recv.at[at], (g, at)).wait()

    copy_c = pltpu.make_async_copy(codes, idx, local_sem.at[5])
    copy_c.start()
    copy_c.wait()
    copy_h.wait()
    halos(0)

    def build(r):
        @pl.loop(0, slots)
        def _(j):
            src, k = j // sc, j % sc
            keep = jnp.where(idx[src, 0, r * sc + k] >= 0, 1.0, 0.0).astype(jnp.float32)
            hr = (hrecv[src, r, k, 0].astype(jnp.float32) * keep).astype(jnp.bfloat16)
            hi = (hrecv[src, r, k, 1].astype(jnp.float32) * keep).astype(jnp.bfloat16)
            first = pl.ds(pl.multiple_of(j * 2 * bs, bs), bs)
            second = pl.ds(pl.multiple_of(j * 2 * bs + bs, bs), bs)
            hc[r, 0:bs, first] = hr
            hc[r, 0:bs, second] = -hi
            hc[r, bs : 2 * bs, first] = hi
            hc[r, bs : 2 * bs, second] = hr

    group = min(GROUP, slots)

    def panel(r, j):
        at = idx[j // sc, 0, r * sc + j % sc]
        return jnp.where(at >= 0, at, rb)

    def product(n, r):
        def part(p):
            base = p * group
            rhs = jnp.concatenate(
                [bufs[n - 1][panel(r, base + u)] for u in range(group)], axis=0
            )
            lhs = hc[r, :, pl.ds(pl.multiple_of(base * 2 * bs, 2 * bs), group * 2 * bs)]
            return jnp.dot(lhs, rhs, preferred_element_type=jnp.float32)

        if slots == group:
            return part(0)
        zero = jnp.zeros((2 * bs, width), jnp.float32)
        return lax.fori_loop(0, slots // group, lambda p, a: a + part(p), zero)

    for n in range(1, STEPS + 1):
        @pl.loop(0, R)
        def _(r, n=n):
            if n == 1:
                @pl.loop(1, ns)
                def _(d):
                    arrived(d, r).wait_recv()

                @pl.when(r + ahead < R)
                def _():
                    @pl.loop(1, ns)
                    def _(d):
                        coupling(d, r).wait_send()

                    @pl.loop(1, ns)
                    def _(d):
                        coupling(d, r + ahead).start()

                build(r)
            t = product(n, r)
            if n > 1:
                t = 2.0 * t - tbuf[n % 2, r]
            tbuf[n % 2, r] = t
            c = s * R + r
            if n == STEPS:
                bufs[n][c] = t.astype(jnp.bfloat16)
            else:
                bufs[n][rb + c] = t.astype(jnp.bfloat16)
            each(n, c, lambda x: x.start())
            moment(n, r, t)

        if n == STEPS:
            msec[s] = mloc[...]

            @pl.loop(1, ns)
            def _(d):
                to = lax.rem(s + d, ns)
                remote(mloc, msec.at[s], m_send.at[to], m_recv.at[s], (g, to)).start()

        @pl.loop(1, ns)
        def _(d, n=n):
            @pl.loop(0, R)
            def _(r):
                @pl.when(s - d >= 0)
                def _():
                    c = (s - d) * R + r
                    up(n, c).wait_recv()
                    each(n, c, lambda x: x.start())

                @pl.when(s + d < ns)
                def _():
                    c = (s + d) * R + r
                    down(n, c).wait_recv()
                    each(n, c, lambda x: x.start())

        if n < STEPS:
            halos(n)
        if n == STEPS - 1:
            pltpu.make_async_copy(ext3.at[pl.ds(rb, rb)], t3_out, local_sem.at[2]).start()

    copy_t = pltpu.make_async_copy(last, t4_out, local_sem.at[3])
    copy_t.start()

    @pl.loop(1, ns)
    def _(d):
        at = lax.rem(s + d, ns)
        remote(mloc, msec.at[at], m_send.at[at], m_recv.at[at], (g, at)).wait()

    total = msec[0]
    for i in range(1, ns):
        total += msec[i]
    mrow[g] = total

    @pl.loop(1, nr)
    def _(d):
        to = lax.rem(g + d, nr)
        remote(mrow.at[g], mrow.at[g], n_send.at[to], n_recv.at[g], (to, s)).start()

    @pl.loop(1, nr)
    def _(d):
        at = lax.rem(g + d, nr)
        remote(mrow.at[at], mrow.at[at], n_send.at[at], n_recv.at[at], (at, s)).wait()

    total = mrow[0]
    for i in range(1, nr):
        total += mrow[i]
    mom_out[...] = total * scale

    for r in range(R - ahead, R):
        @pl.loop(1, ns)
        def _(d, r=r):
            coupling(d, r).wait_send()

    for n in range(STEPS + 1):
        @pl.loop(0, rb)
        def _(c, n=n):
            each(n, c, lambda x: x.wait_send())

    pltpu.make_async_copy(ext3.at[pl.ds(rb, rb)], t3_out, local_sem.at[2]).wait()
    copy_t.wait()


def widen(bs, t4, t3, last_vec, before_vec):
    for src, dst in ((t4, last_vec), (t3, before_vec)):
        for i in range(src.shape[0]):
            for q in range(2):
                part = src[i, q * bs : (q + 1) * bs, :]
                dst[i * bs : (i + 1) * bs, q, :] = part.astype(jnp.float32)


def body(nr, ns, start_vec, left_vec, hamil, cols, live):
    rb, sc = cols.shape
    bs = hamil.shape[-1]
    width = start_vec.shape[-1]
    R = rb // ns
    slots = sc * ns
    base = lax.axis_index("rows") * rb
    scale = 1.0 / (2.0 * bs * rb) ** 0.5

    mask = jnp.arange(sc)[None, :] < live
    code = jnp.where(mask, cols - base + rb, -1).reshape(ns, 1, R * sc)
    code = jnp.pad(code, ((0, 0), (0, 7), (0, -(R * sc) % 128)), constant_values=-1)

    dma = pltpu.SemaphoreType.DMA
    vmem = pl.BlockSpec(memory_space=pltpu.VMEM)
    anywhere = pl.BlockSpec(memory_space=pl.ANY)
    bf, f32 = jnp.bfloat16, jnp.float32
    ext = pltpu.VMEM((3 * rb, 2 * bs, width), bf)
    mom, t3, t4 = pl.pallas_call(
        functools.partial(kernel, nr, ns, slots, scale),
        out_shape=(
            jax.ShapeDtypeStruct((8, width), f32),
            jax.ShapeDtypeStruct((rb, 2 * bs, width), bf),
            jax.ShapeDtypeStruct((rb, 2 * bs, width), bf),
        ),
        in_specs=[vmem, anywhere, anywhere, anywhere],
        out_specs=(vmem, anywhere, anywhere),
        scratch_shapes=[
            pltpu.VMEM(start_vec.shape, f32),
            pltpu.VMEM((R * bs, 2, width), f32),
            pltpu.VMEM(code.shape, jnp.int32),
            pltpu.SMEM(code.shape, jnp.int32),
            ext, ext, ext, ext,
            pltpu.VMEM((rb, 2 * bs, width), bf),
            pltpu.VMEM((ns, R, sc, 2, bs, bs), bf),
            pltpu.VMEM((R, 2 * bs, slots * 2 * bs), bf),
            pltpu.VMEM((2, R, 2 * bs, width), f32),
            pltpu.VMEM((R, 2 * bs, width), f32),
            pltpu.VMEM((8, width), f32),
            pltpu.VMEM((ns, 8, width), f32),
            pltpu.VMEM((nr, 8, width), f32),
            dma((STEPS, rb)), dma((STEPS, rb)), dma((STEPS, rb)), dma((STEPS, rb)),
            dma((STEPS, rb)), dma((STEPS, rb)), dma((STEPS, rb)),
            dma((ns, R)), dma((ns, R)), dma((ns,)), dma((ns,)),
            dma((ns,)), dma((ns,)), dma((nr,)), dma((nr,)), dma((6,)),
        ],
        compiler_params=pltpu.CompilerParams(
            collective_id=0, has_side_effects=True, vmem_limit_bytes=56 * 2**20
        ),
    )(code, start_vec, left_vec, hamil)

    taken = pl.BlockSpec((4, 2 * bs, width), lambda b: (b, 0, 0))
    given = pl.BlockSpec((4 * bs, 2, width), lambda b: (b, 0, 0))
    last_vec, before_vec = pl.pallas_call(
        functools.partial(widen, bs),
        out_shape=(jax.ShapeDtypeStruct(start_vec.shape, f32),) * 2,
        grid=(rb // 4,),
        in_specs=[taken, taken],
        out_specs=(given, given),
    )(t4, t3)
    return mom[: STEPS + 1], last_vec, before_vec


def solution(mesh):
    nr, ns = mesh.shape["rows"], mesh.shape["section"]
    return jax.shard_map(
        functools.partial(body, nr, ns),
        mesh=mesh,
        in_specs=(
            P("rows", None, None),
            P("rows", None, None),
            P("rows", "section", None, None, None),
            P("rows", "section"),
            P("rows", "section"),
        ),
        out_specs=(P(), P("rows", None, None), P("rows", None, None)),
        check_vma=False,
    )
```

```python
import functools

import jax
import jax.numpy as jnp
from jax import lax
from jax.experimental import pallas as pl
from jax.experimental.pallas import tpu as pltpu
from jax.sharding import PartitionSpec as P

MESH = pl.DeviceIdType.MESH
STEPS = 4
GROUP = 16


def kernel(
    nr, ns, slots, scale,
    code, start_hbm, left_hbm, hm,
    mom_out, t3_out, t4_out,
    stage, left_stage, codes, idx, ext0, ext1, ext2, ext3, last, hrecv, hc, tbuf, left, mloc, msec, mrow,
    up_sem, down_sem, right_sem, left_sem, own_recv, lhalo_recv, rhalo_recv,
    h_send, h_recv, c_send, c_recv, m_send, m_recv, n_send, n_recv, local_sem,
):
    g = lax.axis_index("rows")
    s = lax.axis_index("section")
    rb = hm.shape[0]
    width = start_hbm.shape[-1]
    R = rb // ns
    bs = hm.shape[-1]
    sc = hm.shape[1]
    bufs = (ext0, ext1, ext2, ext3, last)

    barrier = pltpu.get_barrier_semaphore()

    @pl.loop(1, ns)
    def _(d):
        pl.semaphore_signal(barrier, inc=1, device_id=(g, lax.rem(s + d, ns)), device_id_type=MESH)

    @pl.loop(1, nr)
    def _(d):
        pl.semaphore_signal(barrier, inc=1, device_id=(lax.rem(g + d, nr), s), device_id_type=MESH)

    pl.semaphore_wait(barrier, ns + nr - 2)

    def own(n, c):
        return bufs[n].at[c] if n == STEPS else bufs[n].at[rb + c]

    def remote(src, dst, ss, rs, dev):
        return pltpu.make_async_remote_copy(
            src_ref=src, dst_ref=dst, send_sem=ss, recv_sem=rs, device_id=dev, device_id_type=MESH
        )

    def up(n, c):
        return remote(own(n, c), own(n, c), up_sem.at[n - 1, c], own_recv.at[n - 1, c], (g, s + 1))

    def down(n, c):
        return remote(own(n, c), own(n, c), down_sem.at[n - 1, c], own_recv.at[n - 1, c], (g, s - 1))

    def right(n, c):
        return remote(own(n, c), bufs[n].at[c], right_sem.at[n, c], lhalo_recv.at[n, c], (g + 1, s))

    def leftward(n, c):
        return remote(own(n, c), bufs[n].at[2 * rb + c], left_sem.at[n, c], rhalo_recv.at[n, c], (g - 1, s))

    def each(n, c, act):
        k = c // R
        if n > 0:
            @pl.when((k <= s) & (s < ns - 1))
            def _():
                act(up(n, c))

            @pl.when((k >= s) & (s > 0))
            def _():
                act(down(n, c))
        if n < STEPS:
            @pl.when((k >= s) & (g < nr - 1))
            def _():
                act(right(n, c))

            @pl.when((k <= s) & (g > 0))
            def _():
                act(leftward(n, c))

    def halos(n):
        @pl.loop(0, rb)
        def _(c):
            k = c // R

            @pl.when((k >= s) & (g > 0))
            def _():
                right(n, c).wait_recv()

            @pl.when((k <= s) & (g < nr - 1))
            def _():
                leftward(n, c).wait_recv()

    def coupling(d, r):
        to = lax.rem(s + d, ns)
        return remote(hm.at[to * R + r], hrecv.at[s, r], h_send.at[to, r], h_recv.at[s, r], (g, to))

    def arrived(d, r):
        at = lax.rem(s + d, ns)
        return remote(hm.at[r], hrecv.at[at, r], h_send.at[at, r], h_recv.at[at, r], (g, at))

    @pl.loop(1, ns)
    def _(d):
        to = lax.rem(s + d, ns)
        remote(code.at[to], codes.at[s], c_send.at[to], c_recv.at[s], (g, to)).start()

    ahead = min(4, R)
    for r in range(ahead):
        @pl.loop(1, ns)
        def _(d, r=r):
            coupling(ns - d, r).start()

    copy_v = pltpu.make_async_copy(start_hbm, stage, local_sem.at[1])
    copy_v.start()
    copy_l = pltpu.make_async_copy(
        left_hbm.at[pl.ds(s * (R * bs), R * bs)], left_stage, local_sem.at[4]
    )
    copy_l.start()
    copy_h = pltpu.make_async_copy(hm.at[pl.ds(s * R, R)], hrecv.at[s], local_sem.at[0])
    copy_h.start()
    mloc[...] = jnp.zeros_like(mloc)
    codes[s] = code[s]
    copy_v.wait()

    @pl.loop(0, rb)
    def _(c):
        for q in range(2):
            part = stage[pl.ds(c * bs, bs), q, :]
            ext0[rb + c, q * bs : (q + 1) * bs, :] = part.astype(jnp.bfloat16)
        each(0, c, lambda x: x.start())

    copy_l.wait()

    def moment(n, r, t):
        for q in range(2):
            probe = left[r, q * bs : (q + 1) * bs, :]
            mloc[n : n + 1, :] += jnp.sum(probe * t[q * bs : (q + 1) * bs], axis=0, keepdims=True)

    @pl.loop(0, R)
    def _(r):
        for q in range(2):
            rows = slice(q * bs, (q + 1) * bs)
            tbuf[0, r, rows, :] = stage[pl.ds((s * R + r) * bs, bs), q, :]
            left[r, rows, :] = left_stage[pl.ds(r * bs, bs), q, :]
        moment(0, r, tbuf[0, r])

    @pl.loop(1, ns)
    def _(d):
        at = lax.rem(s + d, ns)
        remote(code.at[at], codes.at[at], c_send.at[at], c_recv.at[at], (g, at)).wait()

    copy_c = pltpu.make_async_copy(codes, idx, local_sem.at[5])
    copy_c.start()
    copy_c.wait()
    copy_h.wait()
    halos(0)

    def build(r):
        @pl.loop(0, slots)
        def _(j):
            src, k = j // sc, j % sc
            keep = jnp.where(idx[src, 0, r * sc + k] >= 0, 1.0, 0.0).astype(jnp.float32)
            hr = (hrecv[src, r, k, 0].astype(jnp.float32) * keep).astype(jnp.bfloat16)
            hi = (hrecv[src, r, k, 1].astype(jnp.float32) * keep).astype(jnp.bfloat16)
            first = pl.ds(pl.multiple_of(j * 2 * bs, bs), bs)
            second = pl.ds(pl.multiple_of(j * 2 * bs + bs, bs), bs)
            hc[r, 0:bs, first] = hr
            hc[r, 0:bs, second] = -hi
            hc[r, bs : 2 * bs, first] = hi
            hc[r, bs : 2 * bs, second] = hr

    group = min(GROUP, slots)

    def panel(r, j):
        at = idx[j // sc, 0, r * sc + j % sc]
        return jnp.where(at >= 0, at, rb)

    def product(n, r):
        def part(p):
            base = p * group
            rhs = jnp.concatenate(
                [bufs[n - 1][panel(r, base + u)] for u in range(group)], axis=0
            )
            lhs = hc[r, :, pl.ds(pl.multiple_of(base * 2 * bs, 2 * bs), group * 2 * bs)]
            return jnp.dot(lhs, rhs, preferred_element_type=jnp.float32)

        if slots == group:
            return part(0)
        zero = jnp.zeros((2 * bs, width), jnp.float32)
        return lax.fori_loop(0, slots // group, lambda p, a: a + part(p), zero)

    def gather(n, low, high):
        @pl.loop(low, high)
        def _(d):
            @pl.loop(0, R)
            def _(r):
                @pl.when(s - d >= 0)
                def _():
                    c = (s - d) * R + r
                    up(n, c).wait_recv()
                    each(n, c, lambda x: x.start())

                @pl.when(s + d < ns)
                def _():
                    c = (s + d) * R + r
                    down(n, c).wait_recv()
                    each(n, c, lambda x: x.start())

                if n < STEPS:
                    @pl.when(d == 1)
                    def _():
                        moment(n, r, tbuf[n % 2, r])

    for n in range(1, STEPS + 1):
        @pl.loop(0, R)
        def _(r, n=n):
            if n == 1:
                @pl.loop(1, ns)
                def _(d):
                    arrived(d, r).wait_recv()

                @pl.when(r + ahead < R)
                def _():
                    @pl.loop(1, ns)
                    def _(d):
                        coupling(d, r).wait_send()

                    @pl.loop(1, ns)
                    def _(d):
                        coupling(d, r + ahead).start()

                build(r)
            t = product(n, r)
            if n > 1:
                t = 2.0 * t - tbuf[n % 2, r]
            tbuf[n % 2, r] = t
            c = s * R + r
            if n == STEPS:
                bufs[n][c] = t.astype(jnp.bfloat16)
            else:
                bufs[n][rb + c] = t.astype(jnp.bfloat16)
            each(n, c, lambda x: x.start())
            if n == STEPS:
                moment(n, r, t)

        if n == STEPS:
            msec[s] = mloc[...]

            @pl.loop(1, ns)
            def _(d):
                to = lax.rem(s + d, ns)
                remote(mloc, msec.at[s], m_send.at[to], m_recv.at[s], (g, to)).start()

        if n < STEPS:
            gather(n, 1, ns)
            halos(n)
        if n == STEPS - 1:
            pltpu.make_async_copy(ext3.at[pl.ds(rb, rb)], t3_out, local_sem.at[2]).start()

    gather(STEPS, 1, ns - 1)

    @pl.loop(1, ns)
    def _(d):
        at = lax.rem(s + d, ns)
        remote(mloc, msec.at[at], m_send.at[at], m_recv.at[at], (g, at)).wait()

    total = msec[0]
    for i in range(1, ns):
        total += msec[i]
    mrow[g] = total

    @pl.loop(1, nr)
    def _(d):
        to = lax.rem(g + d, nr)
        remote(mrow.at[g], mrow.at[g], n_send.at[to], n_recv.at[g], (to, s)).start()

    gather(STEPS, ns - 1, ns)
    copy_t = pltpu.make_async_copy(last, t4_out, local_sem.at[3])
    copy_t.start()

    @pl.loop(1, nr)
    def _(d):
        at = lax.rem(g + d, nr)
        remote(mrow.at[at], mrow.at[at], n_send.at[at], n_recv.at[at], (at, s)).wait()

    total = mrow[0]
    for i in range(1, nr):
        total += mrow[i]
    mom_out[...] = total * scale

    for r in range(R - ahead, R):
        @pl.loop(1, ns)
        def _(d, r=r):
            coupling(d, r).wait_send()

    for n in range(STEPS + 1):
        @pl.loop(0, rb)
        def _(c, n=n):
            each(n, c, lambda x: x.wait_send())

    pltpu.make_async_copy(ext3.at[pl.ds(rb, rb)], t3_out, local_sem.at[2]).wait()
    copy_t.wait()


def widen(bs, t4, t3, last_vec, before_vec):
    for src, dst in ((t4, last_vec), (t3, before_vec)):
        for i in range(src.shape[0]):
            for q in range(2):
                part = src[i, q * bs : (q + 1) * bs, :]
                dst[i * bs : (i + 1) * bs, q, :] = part.astype(jnp.float32)


def body(nr, ns, start_vec, left_vec, hamil, cols, live):
    rb, sc = cols.shape
    bs = hamil.shape[-1]
    width = start_vec.shape[-1]
    R = rb // ns
    slots = sc * ns
    base = lax.axis_index("rows") * rb
    scale = 1.0 / (2.0 * bs * rb) ** 0.5

    mask = jnp.arange(sc)[None, :] < live
    code = jnp.where(mask, cols - base + rb, -1).reshape(ns, 1, R * sc)
    code = jnp.pad(code, ((0, 0), (0, 7), (0, -(R * sc) % 128)), constant_values=-1)

    dma = pltpu.SemaphoreType.DMA
    vmem = pl.BlockSpec(memory_space=pltpu.VMEM)
    anywhere = pl.BlockSpec(memory_space=pl.ANY)
    bf, f32 = jnp.bfloat16, jnp.float32
    ext = pltpu.VMEM((3 * rb, 2 * bs, width), bf)
    mom, t3, t4 = pl.pallas_call(
        functools.partial(kernel, nr, ns, slots, scale),
        out_shape=(
            jax.ShapeDtypeStruct((8, width), f32),
            jax.ShapeDtypeStruct((rb, 2 * bs, width), bf),
            jax.ShapeDtypeStruct((rb, 2 * bs, width), bf),
        ),
        in_specs=[vmem, anywhere, anywhere, anywhere],
        out_specs=(vmem, anywhere, anywhere),
        scratch_shapes=[
            pltpu.VMEM(start_vec.shape, f32),
            pltpu.VMEM((R * bs, 2, width), f32),
            pltpu.VMEM(code.shape, jnp.int32),
            pltpu.SMEM(code.shape, jnp.int32),
            ext, ext, ext, ext,
            pltpu.VMEM((rb, 2 * bs, width), bf),
            pltpu.VMEM((ns, R, sc, 2, bs, bs), bf),
            pltpu.VMEM((R, 2 * bs, slots * 2 * bs), bf),
            pltpu.VMEM((2, R, 2 * bs, width), f32),
            pltpu.VMEM((R, 2 * bs, width), f32),
            pltpu.VMEM((8, width), f32),
            pltpu.VMEM((ns, 8, width), f32),
            pltpu.VMEM((nr, 8, width), f32),
            dma((STEPS, rb)), dma((STEPS, rb)), dma((STEPS, rb)), dma((STEPS, rb)),
            dma((STEPS, rb)), dma((STEPS, rb)), dma((STEPS, rb)),
            dma((ns, R)), dma((ns, R)), dma((ns,)), dma((ns,)),
            dma((ns,)), dma((ns,)), dma((nr,)), dma((nr,)), dma((6,)),
        ],
        compiler_params=pltpu.CompilerParams(
            collective_id=0, has_side_effects=True, vmem_limit_bytes=56 * 2**20
        ),
    )(code, start_vec, left_vec, hamil)

    taken = pl.BlockSpec((4, 2 * bs, width), lambda b: (b, 0, 0))
    given = pl.BlockSpec((4 * bs, 2, width), lambda b: (b, 0, 0))
    last_vec, before_vec = pl.pallas_call(
        functools.partial(widen, bs),
        out_shape=(jax.ShapeDtypeStruct(start_vec.shape, f32),) * 2,
        grid=(rb // 4,),
        in_specs=[taken, taken],
        out_specs=(given, given),
    )(t4, t3)
    return mom[: STEPS + 1], last_vec, before_vec


def solution(mesh):
    nr, ns = mesh.shape["rows"], mesh.shape["section"]
    return jax.shard_map(
        functools.partial(body, nr, ns),
        mesh=mesh,
        in_specs=(
            P("rows", None, None),
            P("rows", None, None),
            P("rows", "section", None, None, None),
            P("rows", "section"),
            P("rows", "section"),
        ),
        out_specs=(P(), P("rows", None, None), P("rows", None, None)),
        check_vma=False,
    )
```
